32 devices in a mesh: groups: 2 (over y), tm: 4 (over z), row: 2 (over core), col: 2 (over x).
Axes of the slice: x: 2, y: 2, z: 4, core: 2. Of those that a mesh axis runs over, the one named last changes fastest.
Arguments:
- raw_traces: bfloat16 [64, 144, 10240], P('tm', None, ('groups', 'row', 'col')), parts along dimension 2, may hold values from -6 to 6
- window_offsets: int32 [128], P(('groups', 'tm')), parts along dimension 0, may hold values from 0 to 16, as said below
- dead_channels: int32 [256], P('groups'), parts along dimension 0, may hold values from 0 to 5119, as said below
Outputs:
- cross_spectra: bfloat16 [2, 4, 10240, 5120], P(None, None, ('groups', 'tm', 'row'), 'col'), parts along dimension 2
The draws below stay inside these ranges and needn't reach their ends.
There are 2 independent parts, one for each index of `groups`. The reference program is written for one: setup_inputs(seed, part) draws one part's arguments, and reference() takes and returns one part's arrays. A program takes and returns all parts, laid end to end along the dimension named above; each array names one. Nothing has to cross between parts.
Inputs may be any that keep to these rules, and one draw needn't show every extreme that they name: `window_offsets`: some window starts at 0 and some at 16. `dead_channels`: distinct channel numbers; channels 0 and 5119 are always dead.
All inputs are finite; a program needn't handle non-finite values.
Results may differ from the reference program's by a relative error of at most 0.0071.
Values may be sent and summed in bfloat16 or wider, within the bound.
No kernel may reach another device: no remote copies, remote signals or barrier semaphores. Data moves between devices by JAX's collectives and lax.ppermute only.
A program may use at most 192 MiB of HBM per device.

```python
import math
import jax
import jax.numpy as jnp
from jax import lax

C = 5120
L = 128
PAD = 16
F = 4
NDEAD = 128
WINDOWS = 64


def draw_window_offsets(key, part):
    first, second = jax.random.split(jax.random.fold_in(key, 11))
    values = jax.random.randint(first, (WINDOWS,), 0, PAD + 1)
    place = jax.random.randint(second, (), 0, WINDOWS)
    values = values.at[place].set(PAD)
    values = values.at[(place + 1) % WINDOWS].set(0)
    return values.astype(jnp.int32)


def draw_dead_channels(key, part):
    shuffled = jax.random.permutation(jax.random.fold_in(key, 23), C - 2) + 1
    first_one = jnp.zeros((1,), jnp.int32)
    last_one = jnp.full((1,), C - 1, jnp.int32)
    return jnp.concatenate([first_one, shuffled[:NDEAD - 2].astype(jnp.int32), last_one]).astype(jnp.int32)


def steps_of(key, dims, shards, least, high):
    level = 1.0
    for position, parts in shards:
        draws = jax.random.uniform(jax.random.fold_in(jax.random.fold_in(key, 6), position), (parts,), jnp.float32, least / len(shards), high / len(shards))
        level = level * jnp.repeat(jnp.exp(draws), dims[position] // parts).reshape((-1,) + (1,) * (len(dims) - 1 - position))
    return level


def noise(key, shape, spread, reach, cuts=(), held_as=jnp.bfloat16):
    gain = steps_of(key, shape, cuts, -0.22, 0.18) if cuts else 1.0
    result = jax.random.normal(key, shape, jnp.float32) * spread * gain
    return jnp.minimum(jnp.maximum(result, -reach), reach).astype(held_as)


def setup_inputs(seed: int = 0, part: int = 0) -> dict:
    keys = jax.random.split(jax.random.key(seed), 4)
    own_keys = jax.random.split(jax.random.fold_in(keys[3], part), 4)
    return {
        "raw_traces": noise(own_keys[0], (WINDOWS, L + PAD, C), 1.0, 6.0, ((0, 4), (2, 4))),
        "window_offsets": draw_window_offsets(jax.random.fold_in(jax.random.fold_in(keys[3], part), 71), part),
        "dead_channels": draw_dead_channels(jax.random.fold_in(jax.random.fold_in(keys[3], part), 71), part),
    }


def make_table(length):
    sample = jnp.arange(length, dtype=jnp.int32)
    bins = (jnp.arange(F, dtype=jnp.int32) + 1) * (length // 16)
    phase = sample[:, None] * bins[None, :] % length
    angle = 2.0 * math.pi * phase.astype(jnp.float32) / length
    taper = 0.5 - 0.5 * jnp.cos(2.0 * math.pi * sample.astype(jnp.float32) / length)
    weight = taper / math.sqrt(length)
    real_part = weight[:, None] * jnp.cos(angle)
    imag_part = -weight[:, None] * jnp.sin(angle)
    return jnp.concatenate([real_part, imag_part], axis=1).astype(jnp.bfloat16)

def reference(raw_traces, window_offsets, dead_channels):
    table = make_table(L)

    def one_window(window):
        record = lax.dynamic_index_in_dim(raw_traces, window, 0, keepdims=False)
        segment = lax.dynamic_slice_in_dim(record, window_offsets[window].astype(jnp.int32), L, 0)
        return jnp.dot(segment.T, table, preferred_element_type=jnp.float32)
    spectrum = lax.map(one_window, jnp.arange(WINDOWS, dtype=jnp.int32))
    power = lax.optimization_barrier(jnp.mean(spectrum[..., :F] ** 2 + spectrum[..., F:] ** 2, axis=-1))
    channel_ids = jnp.arange(C, dtype=jnp.int32)
    alive = 1.0 - jnp.any(dead_channels[:, None] == channel_ids[None, :], axis=0).astype(jnp.float32)
    factor = lax.rsqrt(jnp.maximum(power, 0.25)) * alive[None, :]
    whitened = (spectrum * factor[..., None]).astype(jnp.bfloat16)
    real_all = whitened[..., :F].astype(jnp.float32)
    imag_all = whitened[..., F:].astype(jnp.float32)
    inverse = 1.0 / WINDOWS

    def one_bin(freq):
        real_cols = lax.dynamic_index_in_dim(real_all, freq, 2, keepdims=False)
        imag_cols = lax.dynamic_index_in_dim(imag_all, freq, 2, keepdims=False)
        high = lax.Precision.HIGHEST
        real_out = jnp.dot(real_cols.T, real_cols, precision=high) + jnp.dot(imag_cols.T, imag_cols, precision=high)
        imag_out = jnp.dot(real_cols.T, imag_cols, precision=high) - jnp.dot(imag_cols.T, real_cols, precision=high)
        return ((real_out * inverse).astype(jnp.bfloat16), (imag_out * inverse).astype(jnp.bfloat16))
    real_stack, imag_stack = lax.map(one_bin, jnp.arange(F, dtype=jnp.int32))
    return jnp.stack([real_stack, imag_stack], axis=0)
```

```python
import functools
import math

import jax
import jax.numpy as jnp
import numpy as np
from jax import lax
from jax.experimental import pallas as pl
from jax.experimental.pallas import tpu as pltpu
from jax.sharding import PartitionSpec as P

L = 128
F = 4
GROUPS = 4
VMEM_LIMIT = 48 * 1024 * 1024


def make_table(length):
    sample = np.arange(length)
    bins = (np.arange(F) + 1) * (length // 16)
    angle = 2.0 * math.pi * (sample[:, None] * bins[None, :] % length) / length
    taper = 0.5 - 0.5 * np.cos(2.0 * math.pi * sample / length)
    weight = taper / math.sqrt(length)
    real_part = weight[:, None] * np.cos(angle)
    imag_part = -weight[:, None] * np.sin(angle)
    table = np.concatenate([real_part, imag_part], axis=1).astype(np.float32)
    return table.astype(jnp.bfloat16)


def spectra_kernel(offsets, table_ref, dead_ref, raw_ref, *rest):
    outs, (shifted, dead_rows, spectrum) = rest[:-3], rest[-3:]
    windows, record_len, width = raw_ref.shape
    step = pl.program_id(0)

    @pl.when(step == 0)
    def _():
        for w in range(windows):
            shifted[w] = pltpu.roll(table_ref[...], offsets[w], 1)
        listed = jnp.broadcast_to(dead_ref[...], (128, dead_ref.shape[1]))
        dead_rows[...] = listed.T

    for w in range(windows):
        lhs = shifted[w][:, :record_len].astype(jnp.bfloat16)
        found = jnp.dot(lhs, raw_ref[w], preferred_element_type=jnp.float32)
        spectrum[:, w, :] = found[: 2 * F]

    power = spectrum[0] * spectrum[0] + spectrum[F] * spectrum[F]
    for f in range(1, F):
        power += spectrum[f] * spectrum[f] + spectrum[F + f] * spectrum[F + f]
    power *= 1.0 / F
    block = lax.axis_index("row") * lax.axis_size("col") + lax.axis_index("col")
    first = (block * pl.num_programs(0) + step) * width
    alive = []
    for part in range(width // 128):
        ids = first + part * 128 + lax.broadcasted_iota(jnp.int32, (1, 128), 1)
        hit = (dead_rows[...] == ids).astype(jnp.float32)
        alive.append(1.0 - jnp.max(hit, axis=0, keepdims=True))
    factor = lax.rsqrt(jnp.maximum(power, 0.25)) * jnp.concatenate(alive, axis=1)
    per = F // len(outs)
    for f in range(F):
        out = outs[f // per]
        for part in range(2):
            white = (spectrum[part * F + f] * factor).astype(jnp.bfloat16)
            out[f % per, part * windows : (part + 1) * windows, :] = white


def spectra(raw_traces, window_offsets, dead_channels, groups):
    windows, record_len, chans = raw_traces.shape
    width = 256 if chans % 256 == 0 else 128
    table = np.zeros((16, 256), np.float32)
    table[: 2 * F, :L] = make_table(L).astype(np.float32).T
    dead = dead_channels.reshape(1, -1)
    per = F // groups
    shape = jax.ShapeDtypeStruct((per, 2 * windows, chans), jnp.bfloat16)
    return pl.pallas_call(
        spectra_kernel,
        grid_spec=pltpu.PrefetchScalarGridSpec(
            num_scalar_prefetch=1,
            grid=(chans // width,),
            in_specs=[
                pl.BlockSpec((16, 256), lambda j, o: (0, 0)),
                pl.BlockSpec(dead.shape, lambda j, o: (0, 0)),
                pl.BlockSpec((windows, record_len, width), lambda j, o: (0, 0, j)),
            ],
            out_specs=[
                pl.BlockSpec((per, 2 * windows, width), lambda j, o: (0, 0, j))
            ]
            * groups,
            scratch_shapes=[
                pltpu.VMEM((windows, 16, 256), jnp.float32),
                pltpu.VMEM((dead.shape[1], 128), jnp.int32),
                pltpu.VMEM((2 * F, windows, width), jnp.float32),
            ],
        ),
        out_shape=[shape] * groups,
        compiler_params=pltpu.CompilerParams(vmem_limit_bytes=VMEM_LIMIT),
        cost_estimate=pl.CostEstimate(
            flops=2 * 16 * windows * record_len * chans,
            bytes_accessed=2 * windows * record_len * chans,
            transcendentals=0,
        ),
        name="spectra",
    )(window_offsets, jnp.asarray(table), dead, raw_traces)


def products_kernel(scale, pieces, spots, *rest):
    mine, (theirs, sent_rows) = rest[:pieces], rest[pieces : pieces + 2]
    out, left = rest[-2:]
    half, tile = pl.program_id(1), pl.program_id(2)
    depth, rows = sent_rows.shape[1:]
    piece = depth // pieces
    width = out.shape[3]

    @pl.when((half == 0) & (tile == 0))
    def _():
        for p in range(pieces):
            real = sent_rows[0, p * piece : p * piece + piece // 2, :].astype(jnp.float32)
            imag = sent_rows[0, p * piece + piece // 2 : (p + 1) * piece, :].astype(jnp.float32)
            at = slice(p * piece, (p + 1) * piece)
            same = jnp.concatenate([real, imag], axis=0)
            crossed = jnp.concatenate([-imag, real], axis=0)
            left[:rows, at] = same.T.astype(jnp.bfloat16)
            left[rows:, at] = crossed.T.astype(jnp.bfloat16)

    columns = pl.ds(pl.multiple_of(tile * width, 128), width)

    def multiply(right):
        found = jnp.dot(left[...], right, preferred_element_type=jnp.float32) * scale
        out[0, 0] = found[:rows].astype(jnp.bfloat16)
        out[1, 0] = found[rows:].astype(jnp.bfloat16)

    @pl.when(half == 0)
    def _():
        multiply(jnp.concatenate([ref[0, :, columns] for ref in mine], axis=0))

    @pl.when(half == 1)
    def _():
        multiply(theirs[0, :, columns])


def products(spots, mine, theirs, rows_in, start, total, target, scale):
    per, depth, chans = theirs.shape
    rows = rows_in.shape[2]
    width = 256
    tiles = chans // width
    piece = mine[0].shape[1]

    def out_map(f, h, j, s):
        return (0, start + f, 0, (h + s[0] - 2 * h * s[0]) * tiles + j)

    in_specs = [pl.BlockSpec((1, piece, chans), lambda f, h, j, s: (f, 0, 0))] * len(mine)
    in_specs += [
        pl.BlockSpec((1, depth, chans), lambda f, h, j, s: (f, 0, 0)),
        pl.BlockSpec((1, depth, rows), lambda f, h, j, s: (f, 0, 0)),
    ]
    args = [spots, *mine, theirs, rows_in]
    aliases = {}
    if target is not None:
        in_specs.append(pl.BlockSpec(memory_space=pl.ANY))
        aliases = {len(args): 0}
        args.append(target)
    return pl.pallas_call(
        functools.partial(products_kernel, scale, len(mine)),
        grid_spec=pltpu.PrefetchScalarGridSpec(
            num_scalar_prefetch=1,
            grid=(per, 2, tiles),
            in_specs=in_specs,
            out_specs=pl.BlockSpec((2, 1, rows, width), out_map),
            scratch_shapes=[pltpu.VMEM((2 * rows, depth), jnp.bfloat16)],
        ),
        out_shape=jax.ShapeDtypeStruct((2, total, rows, 2 * chans), jnp.bfloat16),
        input_output_aliases=aliases,
        compiler_params=pltpu.CompilerParams(vmem_limit_bytes=VMEM_LIMIT),
        cost_estimate=pl.CostEstimate(
            flops=8 * per * rows * depth * chans,
            bytes_accessed=8 * per * rows * chans,
            transcendentals=0,
        ),
        name="products",
    )(*args)


def swap_body(raw_traces, window_offsets, dead_channels):
    nz = lax.axis_size("tm")
    windows = raw_traces.shape[0]
    t, r, c = lax.axis_index("tm"), lax.axis_index("row"), lax.axis_index("col")
    groups = spectra(raw_traces, window_offsets, dead_channels, GROUPS)
    scale = 1.0 / (nz * windows)

    def place(z, row, col):
        return (z * 2 + row) * 2 + col

    def across(apart):
        every = [(z, a, b) for z in range(nz) for a in range(2) for b in range(2)]
        return [(place(z, a, b), place(z ^ apart, b, a)) for z, a, b in every]

    spots = r.reshape(1).astype(jnp.int32)
    half = raw_traces.shape[2] // 2
    result = None
    for g, block in enumerate(groups):
        mine = [lax.ppermute(block, ("tm", "row", "col"), across(d)) for d in range(nz)]
        whole = jnp.concatenate(mine, axis=1)
        theirs = lax.ppermute(whole, "row", [(0, 1), (1, 0)])
        wanted = jnp.where(r == t % 2, whole, theirs)
        held = lax.dynamic_slice_in_dim(wanted, r * half, half, 2)
        passed = lax.ppermute(held, "col", [(0, 1), (1, 0)])
        rows_in = jnp.where(c == t // 2, held, passed)
        result = products(
            spots, mine, theirs, rows_in, g * block.shape[0], F, result, scale
        )
    return result


def contract(left_part, right_part):
    windows_here = left_part.shape[1]
    left_split = left_part.reshape(2, F, windows_here, left_part.shape[2])
    right_split = right_part.reshape(2, F, windows_here, right_part.shape[2])
    real_out = jnp.einsum(
        "cfwi,cfwj->fij", left_split, right_split, preferred_element_type=jnp.float32
    )
    crossed = jnp.stack([right_split[1], -right_split[0]], axis=0)
    imag_out = jnp.einsum("cfwi,cfwj->fij", left_split, crossed, preferred_element_type=jnp.float32)
    return jnp.stack([real_out, imag_out], axis=0)


def gather_body(raw_traces, window_offsets, dead_channels):
    windows, _, chans = raw_traces.shape
    (whole,) = spectra(raw_traces, window_offsets, dead_channels, 1)
    whitened = whole.reshape(F, 2, windows, chans).transpose(1, 0, 2, 3)
    whitened = whitened.reshape(2 * F, windows, chans)
    every_chan = lax.all_gather(whitened, ("row", "col"), axis=2, tiled=True)
    row_pair = lax.all_to_all(every_chan, "tm", split_axis=2, concat_axis=1, tiled=True)
    inverse = 1.0 / row_pair.shape[1]
    col_width = every_chan.shape[2] // lax.axis_size("col")
    col_block = lax.dynamic_slice_in_dim(
        every_chan, lax.axis_index("col") * col_width, col_width, 2
    )
    half_rows = row_pair.shape[2] // lax.axis_size("row")
    row_block = lax.dynamic_slice_in_dim(row_pair, lax.axis_index("row") * half_rows, half_rows, 2)
    total = contract(row_block, lax.all_gather(col_block, "tm", axis=1, tiled=True))
    return (total * inverse).astype(jnp.bfloat16)


def solution(mesh):
    sizes = mesh.shape
    square = sizes["tm"] == 4 and sizes["row"] == 2 and sizes["col"] == 2
    in_specs = (P("tm", None, ("groups", "row", "col")), P(("groups", "tm")), P("groups"))
    out_specs = P(None, None, ("groups", "tm", "row"), "col")
    return jax.shard_map(
        swap_body if square else gather_body,
        mesh=mesh,
        in_specs=in_specs,
        out_specs=out_specs,
        check_vma=False,
    )
```

```python
import functools
import math

import jax
import jax.numpy as jnp
import numpy as np
from jax import lax
from jax.experimental import pallas as pl
from jax.experimental.pallas import tpu as pltpu
from jax.sharding import PartitionSpec as P

L = 128
F = 4
SHARES = 4
SIZES = (2, 2)
VMEM_LIMIT = 48 * 1024 * 1024


def make_table(length):
    sample = np.arange(length)
    bins = (np.arange(F) + 1) * (length // 16)
    angle = 2.0 * math.pi * (sample[:, None] * bins[None, :] % length) / length
    taper = 0.5 - 0.5 * np.cos(2.0 * math.pi * sample / length)
    weight = taper / math.sqrt(length)
    real_part = weight[:, None] * np.cos(angle)
    imag_part = -weight[:, None] * np.sin(angle)
    table = np.concatenate([real_part, imag_part], axis=1).astype(np.float32)
    return table.astype(jnp.bfloat16)


def spectra_kernel(offsets, table_ref, dead_ref, raw_ref, *rest):
    outs, (shifted, dead_rows, spectrum) = rest[:-3], rest[-3:]
    windows, record_len, width = raw_ref.shape
    step = pl.program_id(0)

    @pl.when(step == 0)
    def _():
        for w in range(windows):
            shifted[w] = pltpu.roll(table_ref[...], offsets[w], 1)
        listed = jnp.broadcast_to(dead_ref[...], (128, dead_ref.shape[1]))
        dead_rows[...] = listed.T

    for w in range(windows):
        lhs = shifted[w][:, :record_len].astype(jnp.bfloat16)
        found = jnp.dot(lhs, raw_ref[w], preferred_element_type=jnp.float32)
        spectrum[:, w, :] = found[: 2 * F]

    power = spectrum[0] * spectrum[0] + spectrum[F] * spectrum[F]
    for f in range(1, F):
        power += spectrum[f] * spectrum[f] + spectrum[F + f] * spectrum[F + f]
    power *= 1.0 / F
    block = lax.axis_index("row") * lax.axis_size("col") + lax.axis_index("col")
    first = (block * pl.num_programs(0) + step) * width
    alive = []
    for part in range(width // 128):
        ids = first + part * 128 + lax.broadcasted_iota(jnp.int32, (1, 128), 1)
        hit = (dead_rows[...] == ids).astype(jnp.float32)
        alive.append(1.0 - jnp.max(hit, axis=0, keepdims=True))
    factor = lax.rsqrt(jnp.maximum(power, 0.25)) * jnp.concatenate(alive, axis=1)
    places = [(out, k) for out in outs for k in range(out.shape[0])]
    for f, (out, k) in enumerate(places):
        for part in range(2):
            white = (spectrum[part * F + f] * factor).astype(jnp.bfloat16)
            out[k, part * windows : (part + 1) * windows, :] = white


def spectra(raw_traces, window_offsets, dead_channels, sizes):
    windows, record_len, chans = raw_traces.shape
    width = 256 if chans % 256 == 0 else 128
    table = np.zeros((16, 256), np.float32)
    table[: 2 * F, :L] = make_table(L).astype(np.float32).T
    dead = dead_channels.reshape(1, -1)
    return pl.pallas_call(
        spectra_kernel,
        grid_spec=pltpu.PrefetchScalarGridSpec(
            num_scalar_prefetch=1,
            grid=(chans // width,),
            in_specs=[
                pl.BlockSpec((16, 256), lambda j, o: (0, 0)),
                pl.BlockSpec(dead.shape, lambda j, o: (0, 0)),
                pl.BlockSpec((windows, record_len, width), lambda j, o: (0, 0, j)),
            ],
            out_specs=[
                pl.BlockSpec((per, 2 * windows, width), lambda j, o: (0, 0, j)) for per in sizes
            ],
            scratch_shapes=[
                pltpu.VMEM((windows, 16, 256), jnp.float32),
                pltpu.VMEM((dead.shape[1], 128), jnp.int32),
                pltpu.VMEM((2 * F, windows, width), jnp.float32),
            ],
        ),
        out_shape=[
            jax.ShapeDtypeStruct((per, 2 * windows, chans), jnp.bfloat16) for per in sizes
        ],
        compiler_params=pltpu.CompilerParams(vmem_limit_bytes=VMEM_LIMIT),
        cost_estimate=pl.CostEstimate(
            flops=2 * 16 * windows * record_len * chans,
            bytes_accessed=2 * windows * record_len * chans,
            transcendentals=0,
        ),
        name="spectra",
    )(window_offsets, jnp.asarray(table), dead, raw_traces)


def products_kernel(scale, start, spots, whole, theirs, near, far, *rest):
    out, picked, left, ready, sems = rest[-5:]
    per, depth, chans = whole.shape
    rows = near.shape[2]
    width = ready.shape[3]
    tiles = chans // width
    slots = ready.shape[0]
    f, step = pl.program_id(0), pl.program_id(1)
    count = f * pl.num_programs(1) + step
    own, source = spots[0], spots[1]

    @pl.when(step == 0)
    def _():
        lanes = pl.ds(pl.multiple_of(own * rows, 128), rows)
        for case, take in enumerate(
            (
                lambda: whole[f, :, lanes],
                lambda: theirs[f, :, lanes],
                lambda: near[f],
                lambda: far[f],
            )
        ):

            @pl.when(source == case)
            def _():
                picked[...] = take()

        piece = depth // SHARES
        for p in range(SHARES):
            at = slice(p * piece, (p + 1) * piece)
            real = picked[p * piece : p * piece + piece // 2, :].astype(jnp.float32)
            imag = picked[p * piece + piece // 2 : (p + 1) * piece, :].astype(jnp.float32)
            left[0, :, at] = jnp.concatenate([real, imag], axis=0).T.astype(jnp.bfloat16)
            left[1, :, at] = jnp.concatenate([-imag, real], axis=0).T.astype(jnp.bfloat16)

    second = step // tiles
    tile = step - second * tiles
    slot = lax.rem(count, slots)
    side = own + second - 2 * own * second
    columns = pl.ds(pl.multiple_of(tile * width, 128), width)
    places = pl.ds(pl.multiple_of(side * chans + tile * width, 128), width)

    def store(at):
        return pltpu.make_async_copy(
            ready.at[at], out.at[:, start + f, :, places], sems.at[at]
        )

    @pl.when(count >= slots)
    def _():
        store(slot).wait()

    def multiply(right):
        for part in range(2):
            found = jnp.dot(left[part], right, preferred_element_type=jnp.float32)
            ready[slot, part] = (found * scale).astype(jnp.bfloat16)

    @pl.when(second == 0)
    def _():
        multiply(whole[f, :, columns])

    @pl.when(second == 1)
    def _():
        multiply(theirs[f, :, columns])

    store(slot).start()

    @pl.when(count == per * pl.num_programs(1) - 1)
    def _():
        for at in range(min(slots, per * 2 * tiles)):
            store(at).wait()


def products(spots, whole, theirs, near, far, start, total, target, scale):
    per, depth, chans = whole.shape
    rows = near.shape[2]
    width = chans // 2
    slots = 4
    operands = [whole, theirs, near, far]
    in_specs = [pl.BlockSpec(memory_space=pltpu.VMEM)] * 4
    args = [spots, *operands]
    aliases = {}
    if target is not None:
        in_specs.append(pl.BlockSpec(memory_space=pl.ANY))
        aliases = {len(args): 0}
        args.append(target)
    return pl.pallas_call(
        functools.partial(products_kernel, scale, start),
        grid_spec=pltpu.PrefetchScalarGridSpec(
            num_scalar_prefetch=1,
            grid=(per, 2 * (chans // width)),
            in_specs=in_specs,
            out_specs=pl.BlockSpec(memory_space=pl.ANY),
            scratch_shapes=[
                pltpu.VMEM((depth, rows), jnp.bfloat16),
                pltpu.VMEM((2, rows, depth), jnp.bfloat16),
                pltpu.VMEM((slots, 2, rows, width), jnp.bfloat16),
                pltpu.SemaphoreType.DMA((slots,)),
            ],
        ),
        out_shape=jax.ShapeDtypeStruct((2, total, rows, 2 * chans), jnp.bfloat16),
        input_output_aliases=aliases,
        compiler_params=pltpu.CompilerParams(vmem_limit_bytes=VMEM_LIMIT),
        cost_estimate=pl.CostEstimate(
            flops=8 * per * rows * depth * chans,
            bytes_accessed=8 * per * rows * chans,
            transcendentals=0,
        ),
        name="products",
    )(*args)


def square_body(raw_traces, window_offsets, dead_channels):
    windows, _, chans = raw_traces.shape
    t, r, c = lax.axis_index("tm"), lax.axis_index("row"), lax.axis_index("col")
    scale = 1.0 / (SHARES * windows)
    half = chans // 2
    axes = ("tm", "row", "col")
    corners = [(a, b) for a in range(2) for b in range(2)]

    def place(z, row, col):
        return (z * 2 + row) * 2 + col

    def along(pairs, turned):
        moves = []
        for z, to in pairs:
            for a, b in corners:
                moves.append((place(z, a, b), place(to, b, a) if turned else place(to, a, b)))
        return moves

    def apart(d):
        return [(z, z ^ d) for z in range(SHARES)]

    across, slanted = [], []
    for z in range(SHARES):
        for b in range(2):
            across.append((place(z, z % 2, b), place(z, z % 2, 1 - b)))
            slanted.append((place(z, z % 2, b), place(z, 1 - z % 2, 1 - b)))

    home = (c == t // 2).astype(jnp.int32)
    holder = (r == t % 2).astype(jnp.int32)
    spots = jnp.stack([r, (1 - home) * 2 + 1 - holder]).astype(jnp.int32)
    inner = (t == 1) | (t == 2)

    blocks = spectra(raw_traces, window_offsets, dead_channels, SIZES)
    result, start = None, 0
    for block in blocks:
        here = lax.ppermute(block, axes, along(apart(0), True))
        second = lax.ppermute(block, axes, along(apart(2), True))
        first = lax.ppermute(block, axes, along(apart(1), True))
        middle = lax.ppermute(block, axes, along([(1, 2), (2, 1)], True))
        passed = lax.ppermute(second, axes, along([(2, 3), (1, 0)], False))
        third = jnp.where(inner, middle, passed)
        whole = jnp.concatenate([here, first, second, third], axis=1)
        same = lax.dynamic_slice_in_dim(whole, r * half, half, 2)
        other = lax.dynamic_slice_in_dim(whole, (1 - r) * half, half, 2)
        near = lax.ppermute(same, axes, across)
        far = lax.ppermute(other, axes, slanted)
        theirs = lax.ppermute(whole, "row", [(0, 1), (1, 0)])
        result = products(spots, whole, theirs, near, far, start, F, result, scale)
        start += block.shape[0]
    return result


def contract(left_part, right_part):
    windows_here = left_part.shape[1]
    left_split = left_part.reshape(2, F, windows_here, left_part.shape[2])
    right_split = right_part.reshape(2, F, windows_here, right_part.shape[2])
    real_out = jnp.einsum(
        "cfwi,cfwj->fij", left_split, right_split, preferred_element_type=jnp.float32
    )
    crossed = jnp.stack([right_split[1], -right_split[0]], axis=0)
    imag_out = jnp.einsum("cfwi,cfwj->fij", left_split, crossed, preferred_element_type=jnp.float32)
    return jnp.stack([real_out, imag_out], axis=0)


def gather_body(raw_traces, window_offsets, dead_channels):
    windows, _, chans = raw_traces.shape
    (whole,) = spectra(raw_traces, window_offsets, dead_channels, (F,))
    whitened = whole.reshape(F, 2, windows, chans).transpose(1, 0, 2, 3)
    whitened = whitened.reshape(2 * F, windows, chans)
    every_chan = lax.all_gather(whitened, ("row", "col"), axis=2, tiled=True)
    row_pair = lax.all_to_all(every_chan, "tm", split_axis=2, concat_axis=1, tiled=True)
    inverse = 1.0 / row_pair.shape[1]
    col_width = every_chan.shape[2] // lax.axis_size("col")
    col_block = lax.dynamic_slice_in_dim(
        every_chan, lax.axis_index("col") * col_width, col_width, 2
    )
    half_rows = row_pair.shape[2] // lax.axis_size("row")
    row_block = lax.dynamic_slice_in_dim(row_pair, lax.axis_index("row") * half_rows, half_rows, 2)
    total = contract(row_block, lax.all_gather(col_block, "tm", axis=1, tiled=True))
    return (total * inverse).astype(jnp.bfloat16)


def solution(mesh):
    sizes = mesh.shape
    square = sizes["tm"] == SHARES and sizes["row"] == 2 and sizes["col"] == 2
    in_specs = (P("tm", None, ("groups", "row", "col")), P(("groups", "tm")), P("groups"))
    out_specs = P(None, None, ("groups", "tm", "row"), "col")
    return jax.shard_map(
        square_body if square else gather_body,
        mesh=mesh,
        in_specs=in_specs,
        out_specs=out_specs,
        check_vma=False,
    )
```

```python
import functools
import math

import jax
import jax.numpy as jnp
import numpy as np
from jax import lax
from jax.experimental import pallas as pl
from jax.experimental.pallas import tpu as pltpu
from jax.sharding import PartitionSpec as P

L = 128
F = 4
SHARES = 4
SIZES = (2, 2)
FORWARD = (True, False)
VMEM_LIMIT = 16 * 1024 * 1024
SPECTRA_VMEM = 60 * 1024 * 1024


def make_table(length):
    sample = np.arange(length)
    bins = (np.arange(F) + 1) * (length // 16)
    angle = 2.0 * math.pi * (sample[:, None] * bins[None, :] % length) / length
    taper = 0.5 - 0.5 * np.cos(2.0 * math.pi * sample / length)
    weight = taper / math.sqrt(length)
    real_part = weight[:, None] * np.cos(angle)
    imag_part = -weight[:, None] * np.sin(angle)
    table = np.concatenate([real_part, imag_part], axis=1).astype(np.float32)
    return table.astype(jnp.bfloat16)


def spectra_kernel(offsets_in, table_in, dead_in, raw_in, *rest):
    outs, scratch = rest[:2], rest[2:]
    raw, table, dead, offsets, shifted, spectrum, raw_sems, small_sems = scratch
    steps, windows, record_len, width = raw.shape

    def fetch(step):
        lanes = pl.ds(step * width, width)
        return pltpu.make_async_copy(raw_in.at[:, :, lanes], raw.at[step], raw_sems.at[step])

    small = [
        pltpu.make_async_copy(source, target, small_sems.at[k])
        for k, (source, target) in enumerate(
            ((offsets_in, offsets), (table_in, table), (dead_in, dead))
        )
    ]
    for copy in small:
        copy.start()
    for step in range(steps):
        fetch(step).start()
    for copy in small:
        copy.wait()
    for w in range(windows):
        shifted[w] = pltpu.roll(table[...], offsets[0, w], 1)
    dead_rows = jnp.broadcast_to(dead[...], (128, dead.shape[1])).T
    block = lax.axis_index("row") * lax.axis_size("col") + lax.axis_index("col")

    for step in range(steps):
        fetch(step).wait()
        for w in range(windows):
            lhs = shifted[w][:, :record_len].astype(jnp.bfloat16)
            found = jnp.dot(lhs, raw[step, w], preferred_element_type=jnp.float32)
            spectrum[:, w, :] = found[: 2 * F]
        power = spectrum[0] * spectrum[0] + spectrum[F] * spectrum[F]
        for f in range(1, F):
            power += spectrum[f] * spectrum[f] + spectrum[F + f] * spectrum[F + f]
        power *= 1.0 / F
        first = (block * steps + step) * width
        alive = []
        for part in range(width // 128):
            ids = first + part * 128 + lax.broadcasted_iota(jnp.int32, (1, 128), 1)
            hit = (dead_rows == ids).astype(jnp.float32)
            alive.append(1.0 - jnp.max(hit, axis=0, keepdims=True))
        factor = lax.rsqrt(jnp.maximum(power, 0.25)) * jnp.concatenate(alive, axis=1)
        run = math.gcd(outs[0].shape[3], width)
        for f in range(F):
            for part in range(2):
                white = (spectrum[part * F + f] * factor).astype(jnp.bfloat16)
                at = slice(part * windows, (part + 1) * windows)
                for out in outs:
                    for low in range(0, width if f < out.shape[1] else 0, run):
                        split, lane = divmod(step * width + low, out.shape[3])
                        out[split, f, at, lane : lane + run] = white[:, low : low + run]


def spectra(raw_traces, window_offsets, dead_channels, leading, splits):
    windows, record_len, chans = raw_traces.shape
    width = 256 if chans % 256 == 0 else 128
    steps = chans // width
    table = np.zeros((16, 256), np.float32)
    table[: 2 * F, :L] = make_table(L).astype(np.float32).T
    dead = dead_channels.reshape(1, -1)
    offsets = window_offsets.reshape(1, -1)
    return pl.pallas_call(
        spectra_kernel,
        in_specs=[pl.BlockSpec(memory_space=pltpu.HBM)] * 4,
        out_specs=[pl.BlockSpec(memory_space=pltpu.VMEM)] * 2,
        scratch_shapes=[
            pltpu.VMEM((steps, windows, record_len, width), jnp.bfloat16),
            pltpu.VMEM((16, 256), jnp.float32),
            pltpu.VMEM(dead.shape, jnp.int32),
            pltpu.SMEM(offsets.shape, jnp.int32),
            pltpu.VMEM((windows, 16, 256), jnp.float32),
            pltpu.VMEM((2 * F, windows, width), jnp.float32),
            pltpu.SemaphoreType.DMA((steps,)),
            pltpu.SemaphoreType.DMA((3,)),
        ],
        out_shape=[
            jax.ShapeDtypeStruct((splits, per, 2 * windows, chans // splits), jnp.bfloat16)
            for per in (leading, F)
        ],
        compiler_params=pltpu.CompilerParams(vmem_limit_bytes=SPECTRA_VMEM),
        cost_estimate=pl.CostEstimate(
            flops=2 * 16 * windows * record_len * chans,
            bytes_accessed=2 * windows * record_len * chans,
            transcendentals=0,
        ),
        name="spectra",
    )(offsets, jnp.asarray(table), dead, raw_traces)


def products_kernel(scale, start, spots, whole, theirs, near, far, *rest):
    out, picked, left, ready, sems, pick_sem = rest[-6:]
    splits, per, depth, width = whole.shape
    slots = ready.shape[0]
    f, step = pl.program_id(0), pl.program_id(1)
    count = f * pl.num_programs(1) + step
    own, source = spots[0], spots[1]

    @pl.when(step == 0)
    def _():
        for case, ref in enumerate((whole.at[own, f], theirs.at[own, f], near.at[f], far.at[f])):

            @pl.when(source == case)
            def _():
                pltpu.make_async_copy(ref, picked, pick_sem).start()

        pltpu.make_async_copy(near.at[f], picked, pick_sem).wait()
        piece = depth // SHARES
        for p in range(SHARES):
            at = slice(p * piece, (p + 1) * piece)
            real = picked[p * piece : p * piece + piece // 2, :].astype(jnp.float32)
            imag = picked[p * piece + piece // 2 : (p + 1) * piece, :].astype(jnp.float32)
            left[0, :, at] = jnp.concatenate([real, imag], axis=0).T.astype(jnp.bfloat16)
            left[1, :, at] = jnp.concatenate([-imag, real], axis=0).T.astype(jnp.bfloat16)

    second = step // splits
    tile = step - second * splits
    slot = lax.rem(count, slots)
    side = own + second - 2 * own * second
    places = pl.ds(pl.multiple_of((side * splits + tile) * width, 128), width)

    def store(at):
        return pltpu.make_async_copy(
            ready.at[at], out.at[:, start + f, :, places], sems.at[at]
        )

    @pl.when(count >= slots)
    def _():
        store(slot).wait()

    def multiply(right):
        for part in range(2):
            found = jnp.dot(left[part], right, preferred_element_type=jnp.float32)
            ready[slot, part] = (found * scale).astype(jnp.bfloat16)

    @pl.when(second == 0)
    def _():
        multiply(whole[tile, f])

    @pl.when(second == 1)
    def _():
        multiply(theirs[tile, f])

    store(slot).start()

    @pl.when(count == per * pl.num_programs(1) - 1)
    def _():
        for at in range(min(slots, per * 2 * splits)):
            store(at).wait()


def products(spots, whole, theirs, near, far, start, total, target, scale):
    splits, per, depth, width = whole.shape
    rows, chans = near.shape[2], splits * width
    slots = 4
    operands = [whole, theirs, near, far]
    in_specs = [pl.BlockSpec(memory_space=pltpu.VMEM)] * 2
    in_specs += [pl.BlockSpec(memory_space=pl.ANY)] * 2
    args = [spots, *operands]
    aliases = {}
    if target is not None:
        in_specs.append(pl.BlockSpec(memory_space=pl.ANY))
        aliases = {len(args): 0}
        args.append(target)
    return pl.pallas_call(
        functools.partial(products_kernel, scale, start),
        grid_spec=pltpu.PrefetchScalarGridSpec(
            num_scalar_prefetch=1,
            grid=(per, 2 * splits),
            in_specs=in_specs,
            out_specs=pl.BlockSpec(memory_space=pl.ANY),
            scratch_shapes=[
                pltpu.VMEM((depth, rows), jnp.bfloat16),
                pltpu.VMEM((2, rows, depth), jnp.bfloat16),
                pltpu.VMEM((slots, 2, rows, width), jnp.bfloat16),
                pltpu.SemaphoreType.DMA((slots,)),
                pltpu.SemaphoreType.DMA,
            ],
        ),
        out_shape=jax.ShapeDtypeStruct((2, total, rows, 2 * chans), jnp.bfloat16),
        input_output_aliases=aliases,
        compiler_params=pltpu.CompilerParams(vmem_limit_bytes=VMEM_LIMIT),
        cost_estimate=pl.CostEstimate(
            flops=8 * per * rows * depth * chans,
            bytes_accessed=8 * per * rows * chans,
            transcendentals=0,
        ),
        name="products",
    )(*args)


def square_body(raw_traces, window_offsets, dead_channels):
    windows = raw_traces.shape[0]
    t, r, c = lax.axis_index("tm"), lax.axis_index("row"), lax.axis_index("col")
    scale = 1.0 / (SHARES * windows)
    axes = ("tm", "row", "col")

    def moves(rule):
        def place(z, a, b):
            return (z * 2 + a) * 2 + b

        every = [(z, a, b) for z in range(SHARES) for a in range(2) for b in range(2)]
        return [(place(*at), place(*rule(*at))) for at in every]

    def turned(d):
        return moves(lambda z, a, b: (z ^ d, b, a))

    def apart(d):
        return moves(lambda z, a, b: (z ^ d, a, b))

    def across(z, a, b):
        return (z, a, 1 - b) if (a == z % 2) == (b == z // 2) else (z, 1 - a, b)

    def slanted(z, a, b):
        return (z, 1 - a, 1 - b) if a == z % 2 else (z, 1 - a, b)

    def between(z, a, b):
        return (3 - z, a, b) if z in (1, 2) else (z, 1 - a, b)

    def between_turned(z, a, b):
        return (3 - z, b, a) if z in (1, 2) else (z, 1 - a, b)

    def partner(z, a, b):
        return z, 1 - a, b

    home = (c == t // 2).astype(jnp.int32)
    holder = (r == t % 2).astype(jnp.int32)
    spots = jnp.stack([r, (1 - home) * 2 + 1 - holder]).astype(jnp.int32)

    inner = (t == 1) | (t == 2)

    def share(block, turn, forward):
        move = turned if turn else apart
        second = lax.ppermute(block, axes, move(2))
        first = lax.ppermute(block, axes, move(1))
        if not forward:
            return first, second, lax.ppermute(block, axes, move(3))
        middle = lax.ppermute(block, axes, moves(between_turned if turn else between))
        passed = lax.ppermute(second, axes, apart(1))
        return first, second, jnp.where(inner, middle, passed)

    leading, every = spectra(raw_traces, window_offsets, dead_channels, SIZES[0], 2)
    here_all = lax.ppermute(every, axes, turned(0))
    result, late, start = None, None, 0
    for size, forward in zip(SIZES, FORWARD):
        here = here_all[:, start : start + size]
        pieces = share(leading if start == 0 else here, start == 0, forward)
        whole = jnp.concatenate([here, *pieces], axis=2)
        near = lax.ppermute(whole[r], axes, moves(across))
        far = lax.ppermute(whole[1 - r], axes, moves(slanted))
        theirs = lax.ppermute(whole, axes, moves(partner))
        if late is not None:
            result = products(*late, F, result, scale)
        late = (spots, whole, theirs, near, far, start)
        start += size
    return products(*late, F, result, scale)


def contract(left_part, right_part):
    windows_here = left_part.shape[1]
    left_split = left_part.reshape(2, F, windows_here, left_part.shape[2])
    right_split = right_part.reshape(2, F, windows_here, right_part.shape[2])
    real_out = jnp.einsum(
        "cfwi,cfwj->fij", left_split, right_split, preferred_element_type=jnp.float32
    )
    crossed = jnp.stack([right_split[1], -right_split[0]], axis=0)
    imag_out = jnp.einsum("cfwi,cfwj->fij", left_split, crossed, preferred_element_type=jnp.float32)
    return jnp.stack([real_out, imag_out], axis=0)


def gather_body(raw_traces, window_offsets, dead_channels):
    windows, _, chans = raw_traces.shape
    _, whole = spectra(raw_traces, window_offsets, dead_channels, 1, 1)
    whitened = whole.reshape(F, 2, windows, chans).transpose(1, 0, 2, 3)
    whitened = whitened.reshape(2 * F, windows, chans)
    every_chan = lax.all_gather(whitened, ("row", "col"), axis=2, tiled=True)
    row_pair = lax.all_to_all(every_chan, "tm", split_axis=2, concat_axis=1, tiled=True)
    inverse = 1.0 / row_pair.shape[1]
    col_width = every_chan.shape[2] // lax.axis_size("col")
    col_block = lax.dynamic_slice_in_dim(
        every_chan, lax.axis_index("col") * col_width, col_width, 2
    )
    half_rows = row_pair.shape[2] // lax.axis_size("row")
    row_block = lax.dynamic_slice_in_dim(row_pair, lax.axis_index("row") * half_rows, half_rows, 2)
    total = contract(row_block, lax.all_gather(col_block, "tm", axis=1, tiled=True))
    return (total * inverse).astype(jnp.bfloat16)


def solution(mesh):
    sizes = mesh.shape
    square = sizes["tm"] == SHARES and sizes["row"] == 2 and sizes["col"] == 2
    in_specs = (P("tm", None, ("groups", "row", "col")), P(("groups", "tm")), P("groups"))
    out_specs = P(None, None, ("groups", "tm", "row"), "col")
    return jax.shard_map(
        square_body if square else gather_body,
        mesh=mesh,
        in_specs=in_specs,
        out_specs=out_specs,
        check_vma=False,
    )
```

```python
import functools
import math

import jax
import jax.numpy as jnp
import numpy as np
from jax import lax
from jax.experimental import pallas as pl
from jax.experimental.pallas import tpu as pltpu
from jax.sharding import PartitionSpec as P

L = 128
F = 4
SHARES = 4
SIZES = (2, 2)
FORWARD = (True, False)
VMEM_LIMIT = 20 * 1024 * 1024
SPECTRA_VMEM = 60 * 1024 * 1024


def make_table(length):
    sample = np.arange(length)
    bins = (np.arange(F) + 1) * (length // 16)
    angle = 2.0 * math.pi * (sample[:, None] * bins[None, :] % length) / length
    taper = 0.5 - 0.5 * np.cos(2.0 * math.pi * sample / length)
    weight = taper / math.sqrt(length)
    real_part = weight[:, None] * np.cos(angle)
    imag_part = -weight[:, None] * np.sin(angle)
    table = np.concatenate([real_part, imag_part], axis=1).astype(np.float32)
    return table.astype(jnp.bfloat16)


def spectra_kernel(offsets_in, table_in, dead_in, raw_in, *rest):
    outs, scratch = rest[:2], rest[2:]
    raw, table, dead, offsets, shifted, spectrum, raw_sems, small_sems = scratch
    steps, windows, record_len, width = raw.shape

    def fetch(step):
        lanes = pl.ds(step * width, width)
        return pltpu.make_async_copy(raw_in.at[:, :, lanes], raw.at[step], raw_sems.at[step])

    small = [
        pltpu.make_async_copy(source, target, small_sems.at[k])
        for k, (source, target) in enumerate(
            ((offsets_in, offsets), (table_in, table), (dead_in, dead))
        )
    ]
    for copy in small:
        copy.start()
    for step in range(steps):
        fetch(step).start()
    for copy in small:
        copy.wait()
    for w in range(windows):
        shifted[w] = pltpu.roll(table[...], offsets[0, w], 1)
    dead_rows = jnp.broadcast_to(dead[...], (128, dead.shape[1])).T
    block = lax.axis_index("row") * lax.axis_size("col") + lax.axis_index("col")

    for step in range(steps):
        fetch(step).wait()
        for w in range(windows):
            lhs = shifted[w][:, :record_len].astype(jnp.bfloat16)
            found = jnp.dot(lhs, raw[step, w], preferred_element_type=jnp.float32)
            spectrum[:, w, :] = found[: 2 * F]
        power = spectrum[0] * spectrum[0] + spectrum[F] * spectrum[F]
        for f in range(1, F):
            power += spectrum[f] * spectrum[f] + spectrum[F + f] * spectrum[F + f]
        power *= 1.0 / F
        first = (block * steps + step) * width
        alive = []
        for part in range(width // 128):
            ids = first + part * 128 + lax.broadcasted_iota(jnp.int32, (1, 128), 1)
            hit = (dead_rows == ids).astype(jnp.float32)
            alive.append(1.0 - jnp.max(hit, axis=0, keepdims=True))
        factor = lax.rsqrt(jnp.maximum(power, 0.25)) * jnp.concatenate(alive, axis=1)
        run = math.gcd(outs[0].shape[3], width)
        for f in range(F):
            for part in range(2):
                white = (spectrum[part * F + f] * factor).astype(jnp.bfloat16)
                at = slice(part * windows, (part + 1) * windows)
                for out in outs:
                    for low in range(0, width if f < out.shape[1] else 0, run):
                        split, lane = divmod(step * width + low, out.shape[3])
                        out[split, f, at, lane : lane + run] = white[:, low : low + run]


def spectra(raw_traces, window_offsets, dead_channels, leading, splits):
    windows, record_len, chans = raw_traces.shape
    width = 256 if chans % 256 == 0 else 128
    steps = chans // width
    table = np.zeros((16, 256), np.float32)
    table[: 2 * F, :L] = make_table(L).astype(np.float32).T
    dead = dead_channels.reshape(1, -1)
    offsets = window_offsets.reshape(1, -1)
    return pl.pallas_call(
        spectra_kernel,
        in_specs=[pl.BlockSpec(memory_space=pltpu.HBM)] * 4,
        out_specs=[pl.BlockSpec(memory_space=pltpu.VMEM)] * 2,
        scratch_shapes=[
            pltpu.VMEM((steps, windows, record_len, width), jnp.bfloat16),
            pltpu.VMEM((16, 256), jnp.float32),
            pltpu.VMEM(dead.shape, jnp.int32),
            pltpu.SMEM(offsets.shape, jnp.int32),
            pltpu.VMEM((windows, 16, 256), jnp.float32),
            pltpu.VMEM((2 * F, windows, width), jnp.float32),
            pltpu.SemaphoreType.DMA((steps,)),
            pltpu.SemaphoreType.DMA((3,)),
        ],
        out_shape=[
            jax.ShapeDtypeStruct((splits, per, 2 * windows, chans // splits), jnp.bfloat16)
            for per in (leading, F)
        ],
        compiler_params=pltpu.CompilerParams(vmem_limit_bytes=SPECTRA_VMEM),
        cost_estimate=pl.CostEstimate(
            flops=2 * 16 * windows * record_len * chans,
            bytes_accessed=2 * windows * record_len * chans,
            transcendentals=0,
        ),
        name="spectra",
    )(offsets, jnp.asarray(table), dead, raw_traces)


def products_kernel(scale, start, spots, whole, theirs, near, far, *rest):
    out, picked, left, ready, sems, pick_sems = rest[-6:]
    splits, per, depth, width = whole.shape
    own, source = spots[0], spots[1]

    for case, refs in enumerate((whole.at[own], theirs.at[own], near, far)):

        @pl.when(source == case)
        def _():
            for f in range(per):
                pltpu.make_async_copy(refs.at[f], picked.at[f], pick_sems.at[f]).start()

    def turn(f):
        pltpu.make_async_copy(near.at[f], picked.at[f], pick_sems.at[f]).wait()
        piece = depth // SHARES
        for p in range(SHARES):
            at = slice(p * piece, (p + 1) * piece)
            middle = p * piece + piece // 2
            real = picked[f, p * piece : middle, :].astype(jnp.float32)
            imag = picked[f, middle : (p + 1) * piece, :].astype(jnp.float32)
            left[f, 0, :, at] = jnp.concatenate([real, imag], axis=0).T.astype(jnp.bfloat16)
            left[f, 1, :, at] = jnp.concatenate([-imag, real], axis=0).T.astype(jnp.bfloat16)

    copies = []
    turn(0)
    for f in range(per):
        for second, source_ref in enumerate((whole, theirs)):
            side = own + second - 2 * own * second
            for tile in range(splits):
                slot = (f * 2 + second) * splits + tile
                right = source_ref[tile, f]
                for part in range(2):
                    found = jnp.dot(left[f, part], right, preferred_element_type=jnp.float32)
                    ready[slot, part] = (found * scale).astype(jnp.bfloat16)
                places = pl.ds(pl.multiple_of((side * splits + tile) * width, 128), width)
                copies.append(
                    pltpu.make_async_copy(
                        ready.at[slot], out.at[:, start + f, :, places], sems.at[slot]
                    )
                )
                copies[-1].start()
                if slot == f * 2 * splits and f + 1 < per:
                    turn(f + 1)
    for copy in copies:
        copy.wait()


def products(spots, whole, theirs, near, far, start, total, target, scale):
    splits, per, depth, width = whole.shape
    chans = splits * width
    slots = per * 2 * splits
    in_specs = [pl.BlockSpec(memory_space=pltpu.SMEM)]
    in_specs += [pl.BlockSpec(memory_space=pltpu.VMEM)] * 2
    in_specs += [pl.BlockSpec(memory_space=pl.ANY)] * 2
    args = [spots, whole, theirs, near, far]
    aliases = {}
    if target is not None:
        in_specs.append(pl.BlockSpec(memory_space=pl.ANY))
        aliases = {len(args): 0}
        args.append(target)
    return pl.pallas_call(
        functools.partial(products_kernel, scale, start),
        in_specs=in_specs,
        out_specs=pl.BlockSpec(memory_space=pl.ANY),
        scratch_shapes=[
            pltpu.VMEM((per, depth, width), jnp.bfloat16),
            pltpu.VMEM((per, 2, width, depth), jnp.bfloat16),
            pltpu.VMEM((slots, 2, width, width), jnp.bfloat16),
            pltpu.SemaphoreType.DMA((slots,)),
            pltpu.SemaphoreType.DMA((per,)),
        ],
        out_shape=jax.ShapeDtypeStruct((2, total, width, 2 * chans), jnp.bfloat16),
        input_output_aliases=aliases,
        compiler_params=pltpu.CompilerParams(vmem_limit_bytes=VMEM_LIMIT),
        cost_estimate=pl.CostEstimate(
            flops=8 * per * width * depth * chans,
            bytes_accessed=8 * per * width * chans,
            transcendentals=0,
        ),
        name="products",
    )(*args)


def square_body(raw_traces, window_offsets, dead_channels):
    windows = raw_traces.shape[0]
    t, r, c = lax.axis_index("tm"), lax.axis_index("row"), lax.axis_index("col")
    scale = 1.0 / (SHARES * windows)
    axes = ("tm", "row", "col")

    def moves(rule):
        def place(z, a, b):
            return (z * 2 + a) * 2 + b

        every = [(z, a, b) for z in range(SHARES) for a in range(2) for b in range(2)]
        return [(place(*at), place(*rule(*at))) for at in every]

    def turned(d):
        return moves(lambda z, a, b: (z ^ d, b, a))

    def apart(d):
        return moves(lambda z, a, b: (z ^ d, a, b))

    def across(z, a, b):
        return (z, a, 1 - b) if (a == z % 2) == (b == z // 2) else (z, 1 - a, b)

    def slanted(z, a, b):
        return (z, 1 - a, 1 - b) if a == z % 2 else (z, 1 - a, b)

    def between(z, a, b):
        return (3 - z, a, b) if z in (1, 2) else (z, 1 - a, b)

    def between_turned(z, a, b):
        return (3 - z, b, a) if z in (1, 2) else (z, 1 - a, b)

    def partner(z, a, b):
        return z, 1 - a, b

    source = jnp.where(c == t // 2, jnp.where(r == t % 2, 0, 1), jnp.where(r == t % 2, 2, 3))
    spots = jnp.stack([r, source]).astype(jnp.int32)

    inner = (t == 1) | (t == 2)

    def share(block, turn, forward):
        move = turned if turn else apart
        second = lax.ppermute(block, axes, move(2))
        first = lax.ppermute(block, axes, move(1))
        if not forward:
            return first, second, lax.ppermute(block, axes, move(3))
        middle = lax.ppermute(block, axes, moves(between_turned if turn else between))
        passed = lax.ppermute(second, axes, apart(1))
        return first, second, jnp.where(inner, middle, passed)

    leading, every = spectra(raw_traces, window_offsets, dead_channels, SIZES[0], 2)
    here_all = lax.ppermute(every, axes, turned(0))
    result, late, start = None, None, 0
    for size, forward in zip(SIZES, FORWARD):
        here = here_all[:, start : start + size]
        pieces = share(leading if start == 0 else here, start == 0, forward)
        whole = jnp.concatenate([here, *pieces], axis=2)
        near = lax.ppermute(whole[r], axes, moves(across))
        far = lax.ppermute(whole[1 - r], axes, moves(slanted))
        theirs = lax.ppermute(whole, axes, moves(partner))
        if late is not None:
            result = products(*late, F, result, scale)
        late = [spots, whole, theirs, near, far, start]
        start += size
    return products(*late, F, result, scale)


def contract(left_part, right_part):
    windows_here = left_part.shape[1]
    left_split = left_part.reshape(2, F, windows_here, left_part.shape[2])
    right_split = right_part.reshape(2, F, windows_here, right_part.shape[2])
    real_out = jnp.einsum(
        "cfwi,cfwj->fij", left_split, right_split, preferred_element_type=jnp.float32
    )
    crossed = jnp.stack([right_split[1], -right_split[0]], axis=0)
    imag_out = jnp.einsum("cfwi,cfwj->fij", left_split, crossed, preferred_element_type=jnp.float32)
    return jnp.stack([real_out, imag_out], axis=0)


def gather_body(raw_traces, window_offsets, dead_channels):
    windows, _, chans = raw_traces.shape
    _, whole = spectra(raw_traces, window_offsets, dead_channels, 1, 1)
    whitened = whole.reshape(F, 2, windows, chans).transpose(1, 0, 2, 3)
    whitened = whitened.reshape(2 * F, windows, chans)
    every_chan = lax.all_gather(whitened, ("row", "col"), axis=2, tiled=True)
    row_pair = lax.all_to_all(every_chan, "tm", split_axis=2, concat_axis=1, tiled=True)
    inverse = 1.0 / row_pair.shape[1]
    col_width = every_chan.shape[2] // lax.axis_size("col")
    col_block = lax.dynamic_slice_in_dim(
        every_chan, lax.axis_index("col") * col_width, col_width, 2
    )
    half_rows = row_pair.shape[2] // lax.axis_size("row")
    row_block = lax.dynamic_slice_in_dim(row_pair, lax.axis_index("row") * half_rows, half_rows, 2)
    total = contract(row_block, lax.all_gather(col_block, "tm", axis=1, tiled=True))
    return (total * inverse).astype(jnp.bfloat16)


def solution(mesh):
    sizes = mesh.shape
    square = sizes["tm"] == SHARES and sizes["row"] == 2 and sizes["col"] == 2
    in_specs = (P("tm", None, ("groups", "row", "col")), P(("groups", "tm")), P("groups"))
    out_specs = P(None, None, ("groups", "tm", "row"), "col")
    return jax.shard_map(
        square_body if square else gather_body,
        mesh=mesh,
        in_specs=in_specs,
        out_specs=out_specs,
        check_vma=False,
    )
```

```python
import functools
import math

import jax
import jax.numpy as jnp
import numpy as np
from jax import lax
from jax.experimental import pallas as pl
from jax.experimental.pallas import tpu as pltpu
from jax.sharding import PartitionSpec as P

L = 128
F = 4
SHARES = 4
SIZES = (2, 2)
FORWARD = (True, False)
VMEM_LIMIT = 20 * 1024 * 1024
SPECTRA_VMEM = 60 * 1024 * 1024


def make_table(length):
    sample = np.arange(length)
    bins = (np.arange(F) + 1) * (length // 16)
    angle = 2.0 * math.pi * (sample[:, None] * bins[None, :] % length) / length
    taper = 0.5 - 0.5 * np.cos(2.0 * math.pi * sample / length)
    weight = taper / math.sqrt(length)
    real_part = weight[:, None] * np.cos(angle)
    imag_part = -weight[:, None] * np.sin(angle)
    table = np.concatenate([real_part, imag_part], axis=1).astype(np.float32)
    return table.astype(jnp.bfloat16)


def spectra_kernel(offsets_in, table_in, dead_in, raw_in, *rest):
    outs, scratch = rest[:2], rest[2:]
    raw, table, dead, offsets, shifted, spectrum, raw_sems, small_sems = scratch
    steps, windows, record_len, width = raw.shape

    def fetch(step):
        lanes = pl.ds(step * width, width)
        return pltpu.make_async_copy(raw_in.at[:, :, lanes], raw.at[step], raw_sems.at[step])

    small = [
        pltpu.make_async_copy(source, target, small_sems.at[k])
        for k, (source, target) in enumerate(
            ((offsets_in, offsets), (table_in, table), (dead_in, dead))
        )
    ]
    for copy in small:
        copy.start()
    for step in range(steps):
        fetch(step).start()
    for copy in small:
        copy.wait()
    for w in range(windows):
        shifted[w] = pltpu.roll(table[...], offsets[0, w], 1)
    dead_rows = jnp.broadcast_to(dead[...], (128, dead.shape[1])).T
    block = lax.axis_index("row") * lax.axis_size("col") + lax.axis_index("col")

    for step in range(steps):
        fetch(step).wait()
        for w in range(windows):
            lhs = shifted[w][:, :record_len].astype(jnp.bfloat16)
            found = jnp.dot(lhs, raw[step, w], preferred_element_type=jnp.float32)
            spectrum[:, w, :] = found[: 2 * F]
        power = spectrum[0] * spectrum[0] + spectrum[F] * spectrum[F]
        for f in range(1, F):
            power += spectrum[f] * spectrum[f] + spectrum[F + f] * spectrum[F + f]
        power *= 1.0 / F
        first = (block * steps + step) * width
        alive = []
        for part in range(width // 128):
            ids = first + part * 128 + lax.broadcasted_iota(jnp.int32, (1, 128), 1)
            hit = (dead_rows == ids).astype(jnp.float32)
            alive.append(1.0 - jnp.max(hit, axis=0, keepdims=True))
        factor = lax.rsqrt(jnp.maximum(power, 0.25)) * jnp.concatenate(alive, axis=1)
        run = math.gcd(outs[0].shape[3], width)
        for f in range(F):
            for part in range(2):
                white = (spectrum[part * F + f] * factor).astype(jnp.bfloat16)
                at = slice(part * windows, (part + 1) * windows)
                for out in outs:
                    for low in range(0, width if f < out.shape[1] else 0, run):
                        split, lane = divmod(step * width + low, out.shape[3])
                        out[split, f, at, lane : lane + run] = white[:, low : low + run]


def spectra(raw_traces, window_offsets, dead_channels, leading, splits):
    windows, record_len, chans = raw_traces.shape
    width = 256 if chans % 256 == 0 else 128
    steps = chans // width
    table = np.zeros((16, 256), np.float32)
    table[: 2 * F, :L] = make_table(L).astype(np.float32).T
    dead = dead_channels.reshape(1, -1)
    offsets = window_offsets.reshape(1, -1)
    return pl.pallas_call(
        spectra_kernel,
        in_specs=[pl.BlockSpec(memory_space=pltpu.HBM)] * 4,
        out_specs=[pl.BlockSpec(memory_space=pltpu.VMEM)] * 2,
        scratch_shapes=[
            pltpu.VMEM((steps, windows, record_len, width), jnp.bfloat16),
            pltpu.VMEM((16, 256), jnp.float32),
            pltpu.VMEM(dead.shape, jnp.int32),
            pltpu.SMEM(offsets.shape, jnp.int32),
            pltpu.VMEM((windows, 16, 256), jnp.float32),
            pltpu.VMEM((2 * F, windows, width), jnp.float32),
            pltpu.SemaphoreType.DMA((steps,)),
            pltpu.SemaphoreType.DMA((3,)),
        ],
        out_shape=[
            jax.ShapeDtypeStruct((splits, per, 2 * windows, chans // splits), jnp.bfloat16)
            for per in (leading, F)
        ],
        compiler_params=pltpu.CompilerParams(vmem_limit_bytes=SPECTRA_VMEM),
        cost_estimate=pl.CostEstimate(
            flops=2 * 16 * windows * record_len * chans,
            bytes_accessed=2 * windows * record_len * chans,
            transcendentals=0,
        ),
        name="spectra",
    )(offsets, jnp.asarray(table), dead, raw_traces)


def products_kernel(scale, start, spots, whole, theirs, near, far, *rest):
    out, picked, left, ready, sems, pick_sems = rest[-6:]
    splits, per, depth, width = whole.shape
    own, source = spots[0], spots[1]

    for case, refs in enumerate((whole.at[own], theirs.at[own], near, far)):

        @pl.when(source == case)
        def _():
            for f in range(per):
                pltpu.make_async_copy(refs.at[f], picked.at[f], pick_sems.at[f]).start()

    def turn(f):
        pltpu.make_async_copy(near.at[f], picked.at[f], pick_sems.at[f]).wait()
        piece = depth // SHARES
        for p in range(SHARES):
            at = slice(p * piece, (p + 1) * piece)
            middle = p * piece + piece // 2
            real = picked[f, p * piece : middle, :].astype(jnp.float32)
            imag = picked[f, middle : (p + 1) * piece, :].astype(jnp.float32)
            left[f, 0, :, at] = jnp.concatenate([real, imag], axis=0).T.astype(jnp.bfloat16)
            left[f, 1, :, at] = jnp.concatenate([-imag, real], axis=0).T.astype(jnp.bfloat16)

    copies = []
    turn(0)
    for f in range(per):
        for second, source_ref in enumerate((whole, theirs)):
            side = own + second - 2 * own * second
            for tile in range(splits):
                slot = (f * 2 + second) * splits + tile
                right = source_ref[tile, f]
                for part in range(2):
                    found = jnp.dot(left[f, part], right, preferred_element_type=jnp.float32)
                    ready[slot, part] = (found * scale).astype(jnp.bfloat16)
                places = pl.ds(pl.multiple_of((side * splits + tile) * width, 128), width)
                copies.append(
                    pltpu.make_async_copy(
                        ready.at[slot], out.at[:, start + f, :, places], sems.at[slot]
                    )
                )
                copies[-1].start()
                if slot == f * 2 * splits and f + 1 < per:
                    turn(f + 1)
    for copy in copies:
        copy.wait()


def products(spots, whole, theirs, near, far, start, total, target, scale):
    splits, per, depth, width = whole.shape
    chans = splits * width
    slots = per * 2 * splits
    in_specs = [pl.BlockSpec(memory_space=pltpu.SMEM)]
    in_specs += [pl.BlockSpec(memory_space=pltpu.VMEM)] * 2
    in_specs += [pl.BlockSpec(memory_space=pl.ANY)] * 2
    args = [spots, whole, theirs, near, far]
    aliases = {}
    if target is not None:
        in_specs.append(pl.BlockSpec(memory_space=pl.ANY))
        aliases = {len(args): 0}
        args.append(target)
    return pl.pallas_call(
        functools.partial(products_kernel, scale, start),
        in_specs=in_specs,
        out_specs=pl.BlockSpec(memory_space=pl.ANY),
        scratch_shapes=[
            pltpu.VMEM((per, depth, width), jnp.bfloat16),
            pltpu.VMEM((per, 2, width, depth), jnp.bfloat16),
            pltpu.VMEM((slots, 2, width, width), jnp.bfloat16),
            pltpu.SemaphoreType.DMA((slots,)),
            pltpu.SemaphoreType.DMA((per,)),
        ],
        out_shape=jax.ShapeDtypeStruct((2, total, width, 2 * chans), jnp.bfloat16),
        input_output_aliases=aliases,
        compiler_params=pltpu.CompilerParams(vmem_limit_bytes=VMEM_LIMIT),
        cost_estimate=pl.CostEstimate(
            flops=80 * per * width * depth * chans,
            bytes_accessed=40 * per * width * chans,
            transcendentals=0,
        ),
        name="products",
    )(*args)


def square_body(raw_traces, window_offsets, dead_channels):
    windows = raw_traces.shape[0]
    t, r, c = lax.axis_index("tm"), lax.axis_index("row"), lax.axis_index("col")
    scale = 1.0 / (SHARES * windows)
    axes = ("tm", "row", "col")

    def moves(rule):
        def place(z, a, b):
            return (z * 2 + a) * 2 + b

        every = [(z, a, b) for z in range(SHARES) for a in range(2) for b in range(2)]
        return [(place(*at), place(*rule(*at))) for at in every]

    def turned(d):
        return moves(lambda z, a, b: (z ^ d, b, a))

    def apart(d):
        return moves(lambda z, a, b: (z ^ d, a, b))

    def across(z, a, b):
        return (z, a, 1 - b) if (a == z % 2) == (b == z // 2) else (z, 1 - a, b)

    def slanted(z, a, b):
        return (z, 1 - a, 1 - b) if a == z % 2 else (z, 1 - a, b)

    def between(z, a, b):
        return (3 - z, a, b) if z in (1, 2) else (z, 1 - a, b)

    def between_turned(z, a, b):
        return (3 - z, b, a) if z in (1, 2) else (z, 1 - a, b)

    def partner(z, a, b):
        return z, 1 - a, b

    source = jnp.where(c == t // 2, jnp.where(r == t % 2, 0, 1), jnp.where(r == t % 2, 2, 3))
    spots = jnp.stack([r, source]).astype(jnp.int32)

    inner = (t == 1) | (t == 2)

    def share(block, turn, forward):
        move = turned if turn else apart
        second = lax.ppermute(block, axes, move(2))
        first = lax.ppermute(block, axes, move(1))
        if not forward:
            return first, second, lax.ppermute(block, axes, move(3))
        middle = lax.ppermute(block, axes, moves(between_turned if turn else between))
        passed = lax.ppermute(second, axes, apart(1))
        return first, second, jnp.where(inner, middle, passed)

    leading, every = spectra(raw_traces, window_offsets, dead_channels, SIZES[0], 2)
    opposite = lax.ppermute(every, axes, moves(lambda z, a, b: (z, 1 - a, 1 - b)))
    here_all = jnp.where(r == c, every, opposite)
    result, late, start = None, None, 0
    for size, forward in zip(SIZES, FORWARD):
        here = here_all[:, start : start + size]
        pieces = share(leading if start == 0 else here, start == 0, forward)
        whole = jnp.concatenate([here, *pieces], axis=2)
        near = lax.ppermute(whole[r], axes, moves(across))
        far = lax.ppermute(whole[1 - r], axes, moves(slanted))
        theirs = lax.ppermute(whole, axes, moves(partner))
        if late is not None:
            result = products(*late, F, result, scale)
        late = [spots, whole, theirs, near, far, start]
        start += size
    return products(*late, F, result, scale)


def contract(left_part, right_part):
    windows_here = left_part.shape[1]
    left_split = left_part.reshape(2, F, windows_here, left_part.shape[2])
    right_split = right_part.reshape(2, F, windows_here, right_part.shape[2])
    real_out = jnp.einsum(
        "cfwi,cfwj->fij", left_split, right_split, preferred_element_type=jnp.float32
    )
    crossed = jnp.stack([right_split[1], -right_split[0]], axis=0)
    imag_out = jnp.einsum("cfwi,cfwj->fij", left_split, crossed, preferred_element_type=jnp.float32)
    return jnp.stack([real_out, imag_out], axis=0)


def gather_body(raw_traces, window_offsets, dead_channels):
    windows, _, chans = raw_traces.shape
    _, whole = spectra(raw_traces, window_offsets, dead_channels, 1, 1)
    whitened = whole.reshape(F, 2, windows, chans).transpose(1, 0, 2, 3)
    whitened = whitened.reshape(2 * F, windows, chans)
    every_chan = lax.all_gather(whitened, ("row", "col"), axis=2, tiled=True)
    row_pair = lax.all_to_all(every_chan, "tm", split_axis=2, concat_axis=1, tiled=True)
    inverse = 1.0 / row_pair.shape[1]
    col_width = every_chan.shape[2] // lax.axis_size("col")
    col_block = lax.dynamic_slice_in_dim(
        every_chan, lax.axis_index("col") * col_width, col_width, 2
    )
    half_rows = row_pair.shape[2] // lax.axis_size("row")
    row_block = lax.dynamic_slice_in_dim(row_pair, lax.axis_index("row") * half_rows, half_rows, 2)
    total = contract(row_block, lax.all_gather(col_block, "tm", axis=1, tiled=True))
    return (total * inverse).astype(jnp.bfloat16)


def solution(mesh):
    sizes = mesh.shape
    square = sizes["tm"] == SHARES and sizes["row"] == 2 and sizes["col"] == 2
    in_specs = (P("tm", None, ("groups", "row", "col")), P(("groups", "tm")), P("groups"))
    out_specs = P(None, None, ("groups", "tm", "row"), "col")
    return jax.shard_map(
        square_body if square else gather_body,
        mesh=mesh,
        in_specs=in_specs,
        out_specs=out_specs,
        check_vma=False,
    )
```

```python
import functools
import math

import jax
import jax.numpy as jnp
import numpy as np
from jax import lax
from jax.experimental import pallas as pl
from jax.experimental.pallas import tpu as pltpu
from jax.sharding import PartitionSpec as P

L = 128
F = 4
SHARES = 4
SIZES = (2, 2)
FORWARD = (True, False)
VMEM_LIMIT = 20 * 1024 * 1024
SPECTRA_VMEM = 60 * 1024 * 1024


def make_table(length):
    sample = np.arange(length)
    bins = (np.arange(F) + 1) * (length // 16)
    angle = 2.0 * math.pi * (sample[:, None] * bins[None, :] % length) / length
    taper = 0.5 - 0.5 * np.cos(2.0 * math.pi * sample / length)
    weight = taper / math.sqrt(length)
    real_part = weight[:, None] * np.cos(angle)
    imag_part = -weight[:, None] * np.sin(angle)
    table = np.concatenate([real_part, imag_part], axis=1).astype(np.float32)
    return table.astype(jnp.bfloat16)


def spectra_kernel(offsets_in, table_in, dead_in, raw_in, *rest):
    outs, scratch = rest[:2], rest[2:]
    raw, table, dead, offsets, shifted, spectrum, raw_sems, small_sems = scratch
    steps, windows, record_len, width = raw.shape

    def fetch(step):
        lanes = pl.ds(step * width, width)
        return pltpu.make_async_copy(raw_in.at[:, :, lanes], raw.at[step], raw_sems.at[step])

    small = [
        pltpu.make_async_copy(source, target, small_sems.at[k])
        for k, (source, target) in enumerate(
            ((offsets_in, offsets), (table_in, table), (dead_in, dead))
        )
    ]
    for copy in small:
        copy.start()
    for step in range(steps):
        fetch(step).start()
    for copy in small:
        copy.wait()
    for w in range(windows):
        shifted[w] = pltpu.roll(table[...], offsets[0, w], 1)
    dead_rows = jnp.broadcast_to(dead[...], (128, dead.shape[1])).T
    block = lax.axis_index("row") * lax.axis_size("col") + lax.axis_index("col")

    for step in range(steps):
        fetch(step).wait()
        for w in range(windows):
            lhs = shifted[w][:, :record_len].astype(jnp.bfloat16)
            found = jnp.dot(lhs, raw[step, w], preferred_element_type=jnp.float32)
            spectrum[:, w, :] = found[: 2 * F]
        power = spectrum[0] * spectrum[0] + spectrum[F] * spectrum[F]
        for f in range(1, F):
            power += spectrum[f] * spectrum[f] + spectrum[F + f] * spectrum[F + f]
        power *= 1.0 / F
        first = (block * steps + step) * width
        alive = []
        for part in range(width // 128):
            ids = first + part * 128 + lax.broadcasted_iota(jnp.int32, (1, 128), 1)
            hit = (dead_rows == ids).astype(jnp.float32)
            alive.append(1.0 - jnp.max(hit, axis=0, keepdims=True))
        factor = lax.rsqrt(jnp.maximum(power, 0.25)) * jnp.concatenate(alive, axis=1)
        run = math.gcd(outs[0].shape[3], width)
        for f in range(F):
            for part in range(2):
                white = (spectrum[part * F + f] * factor).astype(jnp.bfloat16)
                at = slice(part * windows, (part + 1) * windows)
                for out in outs:
                    for low in range(0, width if f < out.shape[1] else 0, run):
                        split, lane = divmod(step * width + low, out.shape[3])
                        out[split, f, at, lane : lane + run] = white[:, low : low + run]


def spectra(raw_traces, window_offsets, dead_channels, leading, splits):
    windows, record_len, chans = raw_traces.shape
    width = 256 if chans % 256 == 0 else 128
    steps = chans // width
    table = np.zeros((16, 256), np.float32)
    table[: 2 * F, :L] = make_table(L).astype(np.float32).T
    dead = dead_channels.reshape(1, -1)
    offsets = window_offsets.reshape(1, -1)
    return pl.pallas_call(
        spectra_kernel,
        in_specs=[pl.BlockSpec(memory_space=pltpu.HBM)] * 4,
        out_specs=[pl.BlockSpec(memory_space=pltpu.VMEM)] * 2,
        scratch_shapes=[
            pltpu.VMEM((steps, windows, record_len, width), jnp.bfloat16),
            pltpu.VMEM((16, 256), jnp.float32),
            pltpu.VMEM(dead.shape, jnp.int32),
            pltpu.SMEM(offsets.shape, jnp.int32),
            pltpu.VMEM((windows, 16, 256), jnp.float32),
            pltpu.VMEM((2 * F, windows, width), jnp.float32),
            pltpu.SemaphoreType.DMA((steps,)),
            pltpu.SemaphoreType.DMA((3,)),
        ],
        out_shape=[
            jax.ShapeDtypeStruct((splits, per, 2 * windows, chans // splits), jnp.bfloat16)
            for per in (leading, F)
        ],
        compiler_params=pltpu.CompilerParams(vmem_limit_bytes=SPECTRA_VMEM),
        cost_estimate=pl.CostEstimate(
            flops=2 * 16 * windows * record_len * chans,
            bytes_accessed=2 * windows * record_len * chans,
            transcendentals=0,
        ),
        name="spectra",
    )(offsets, jnp.asarray(table), dead, raw_traces)


def products_kernel(scale, start, spots, whole, theirs, near, far, *rest):
    out, picked, left, ready, sems, pick_sems = rest[-6:]
    splits, per, depth, width = whole.shape
    own, source = spots[0], spots[1]

    for case, refs in enumerate((whole.at[own], theirs.at[own], near, far)):

        @pl.when(source == case)
        def _():
            for f in range(per):
                pltpu.make_async_copy(refs.at[f], picked.at[f], pick_sems.at[f]).start()

    def turn(f):
        pltpu.make_async_copy(near.at[f], picked.at[f], pick_sems.at[f]).wait()
        piece = depth // SHARES
        for p in range(SHARES):
            at = slice(p * piece, (p + 1) * piece)
            middle = p * piece + piece // 2
            real = picked[f, p * piece : middle, :].astype(jnp.float32)
            imag = picked[f, middle : (p + 1) * piece, :].astype(jnp.float32)
            left[f, 0, :, at] = jnp.concatenate([real, imag], axis=0).T.astype(jnp.bfloat16)
            left[f, 1, :, at] = jnp.concatenate([-imag, real], axis=0).T.astype(jnp.bfloat16)

    copies = []
    turn(0)
    for f in range(per):
        for second, source_ref in enumerate((whole, theirs)):
            side = own + second - 2 * own * second
            for tile in range(splits):
                slot = (f * 2 + second) * splits + tile
                right = source_ref[tile, f]
                for part in range(2):
                    found = jnp.dot(left[f, part], right, preferred_element_type=jnp.float32)
                    ready[slot, part] = (found * scale).astype(jnp.bfloat16)
                places = pl.ds(pl.multiple_of((side * splits + tile) * width, 128), width)
                copies.append(
                    pltpu.make_async_copy(
                        ready.at[slot], out.at[:, start + f, :, places], sems.at[slot]
                    )
                )
                copies[-1].start()
                if slot == f * 2 * splits and f + 1 < per:
                    turn(f + 1)
    for copy in copies:
        copy.wait()


def products(spots, whole, theirs, near, far, start, total, target, scale):
    splits, per, depth, width = whole.shape
    chans = splits * width
    slots = per * 2 * splits
    in_specs = [pl.BlockSpec(memory_space=pltpu.SMEM)]
    in_specs += [pl.BlockSpec(memory_space=pltpu.VMEM)] * 2
    in_specs += [pl.BlockSpec(memory_space=pltpu.HBM)] * 2
    args = [spots, whole, theirs, near, far]
    aliases = {}
    if target is not None:
        in_specs.append(pl.BlockSpec(memory_space=pl.ANY))
        aliases = {len(args): 0}
        args.append(target)
    return pl.pallas_call(
        functools.partial(products_kernel, scale, start),
        in_specs=in_specs,
        out_specs=pl.BlockSpec(memory_space=pl.ANY),
        scratch_shapes=[
            pltpu.VMEM((per, depth, width), jnp.bfloat16),
            pltpu.VMEM((per, 2, width, depth), jnp.bfloat16),
            pltpu.VMEM((slots, 2, width, width), jnp.bfloat16),
            pltpu.SemaphoreType.DMA((slots,)),
            pltpu.SemaphoreType.DMA((per,)),
        ],
        out_shape=jax.ShapeDtypeStruct((2, total, width, 2 * chans), jnp.bfloat16),
        input_output_aliases=aliases,
        compiler_params=pltpu.CompilerParams(vmem_limit_bytes=VMEM_LIMIT),
        cost_estimate=pl.CostEstimate(
            flops=80 * per * width * depth * chans,
            bytes_accessed=40 * per * width * chans,
            transcendentals=0,
        ),
        name="products",
    )(*args)


def square_body(raw_traces, window_offsets, dead_channels):
    windows = raw_traces.shape[0]
    t, r, c = lax.axis_index("tm"), lax.axis_index("row"), lax.axis_index("col")
    scale = 1.0 / (SHARES * windows)
    axes = ("tm", "row", "col")

    def moves(rule):
        def place(z, a, b):
            return (z * 2 + a) * 2 + b

        every = [(z, a, b) for z in range(SHARES) for a in range(2) for b in range(2)]
        return [(place(*at), place(*rule(*at))) for at in every]

    def turned(d):
        return moves(lambda z, a, b: (z ^ d, b, a))

    def apart(d):
        return moves(lambda z, a, b: (z ^ d, a, b))

    def across(z, a, b):
        return (z, a, 1 - b) if (a == z % 2) == (b == z // 2) else (z, 1 - a, b)

    def slanted(z, a, b):
        return (z, 1 - a, 1 - b) if a == z % 2 else (z, 1 - a, b)

    def between(z, a, b):
        return (3 - z, a, b) if z in (1, 2) else (z, 1 - a, b)

    def between_turned(z, a, b):
        return (3 - z, b, a) if z in (1, 2) else (z, 1 - a, b)

    def partner(z, a, b):
        return z, 1 - a, b

    source = jnp.where(c == t // 2, jnp.where(r == t % 2, 0, 1), jnp.where(r == t % 2, 2, 3))
    spots = jnp.stack([r, source]).astype(jnp.int32)

    inner = (t == 1) | (t == 2)

    def share(block, turn, forward):
        move = turned if turn else apart
        second = lax.ppermute(block, axes, move(2))
        first = lax.ppermute(block, axes, move(1))
        if not forward:
            return first, second, lax.ppermute(block, axes, move(3))
        middle = lax.ppermute(block, axes, moves(between_turned if turn else between))
        passed = lax.ppermute(second, axes, apart(1))
        return first, second, jnp.where(inner, middle, passed)

    leading, every = spectra(raw_traces, window_offsets, dead_channels, SIZES[0], 2)
    opposite = lax.ppermute(every, axes, moves(lambda z, a, b: (z, 1 - a, 1 - b)))
    here_all = jnp.where(r == c, every, opposite)
    result, late, start = None, None, 0
    for size, forward in zip(SIZES, FORWARD):
        here = here_all[:, start : start + size]
        pieces = share(leading if start == 0 else here, start == 0, forward)
        whole = jnp.concatenate([here, *pieces], axis=2)
        near = lax.ppermute(whole[r], axes, moves(across))
        far = lax.ppermute(whole[1 - r], axes, moves(slanted))
        theirs = lax.ppermute(whole, axes, moves(partner))
        if late is not None:
            result = products(*late, F, result, scale)
        late = [spots, whole, theirs, near, far, start]
        start += size
    return products(*late, F, result, scale)


def contract(left_part, right_part):
    windows_here = left_part.shape[1]
    left_split = left_part.reshape(2, F, windows_here, left_part.shape[2])
    right_split = right_part.reshape(2, F, windows_here, right_part.shape[2])
    real_out = jnp.einsum(
        "cfwi,cfwj->fij", left_split, right_split, preferred_element_type=jnp.float32
    )
    crossed = jnp.stack([right_split[1], -right_split[0]], axis=0)
    imag_out = jnp.einsum("cfwi,cfwj->fij", left_split, crossed, preferred_element_type=jnp.float32)
    return jnp.stack([real_out, imag_out], axis=0)


def gather_body(raw_traces, window_offsets, dead_channels):
    windows, _, chans = raw_traces.shape
    _, whole = spectra(raw_traces, window_offsets, dead_channels, 1, 1)
    whitened = whole.reshape(F, 2, windows, chans).transpose(1, 0, 2, 3)
    whitened = whitened.reshape(2 * F, windows, chans)
    every_chan = lax.all_gather(whitened, ("row", "col"), axis=2, tiled=True)
    row_pair = lax.all_to_all(every_chan, "tm", split_axis=2, concat_axis=1, tiled=True)
    inverse = 1.0 / row_pair.shape[1]
    col_width = every_chan.shape[2] // lax.axis_size("col")
    col_block = lax.dynamic_slice_in_dim(
        every_chan, lax.axis_index("col") * col_width, col_width, 2
    )
    half_rows = row_pair.shape[2] // lax.axis_size("row")
    row_block = lax.dynamic_slice_in_dim(row_pair, lax.axis_index("row") * half_rows, half_rows, 2)
    total = contract(row_block, lax.all_gather(col_block, "tm", axis=1, tiled=True))
    return (total * inverse).astype(jnp.bfloat16)


def solution(mesh):
    sizes = mesh.shape
    square = sizes["tm"] == SHARES and sizes["row"] == 2 and sizes["col"] == 2
    in_specs = (P("tm", None, ("groups", "row", "col")), P(("groups", "tm")), P("groups"))
    out_specs = P(None, None, ("groups", "tm", "row"), "col")
    return jax.shard_map(
        square_body if square else gather_body,
        mesh=mesh,
        in_specs=in_specs,
        out_specs=out_specs,
        check_vma=False,
    )
```
